256 devices in a mesh: row: 16 (over y_lo, x, core), col: 16 (over y_hi, z).
Axes of the slice: x: 4, y: 4 (y_hi: 2, y_lo: 2; y = y_hi * 2 + y_lo), z: 8, core: 2. Of those that a mesh axis runs over, the one named last changes fastest.
Arguments:
- tokens: bfloat16 [2048, 12288], P(('row', 'col')), may hold values from -32 to 32
- norm_gain: float32 [12288], replicated, may hold values from 0.1 to 1.9
- gate_weight: bfloat16 [12288, 12288], P('row', 'col'), may hold values from -0.0546875 to 0.0546875
- up_weight: bfloat16 [12288, 12288], P('row', 'col'), may hold values from -0.0546875 to 0.0546875
- down_weight: bfloat16 [12288, 12288], P('col', 'row'), may hold values from -0.109375 to 0.109375
Outputs:
- block_output: bfloat16 [2048, 12288], P(('row', 'col'))
The draws below stay inside these ranges and needn't reach their ends.
All inputs are finite; a program needn't handle non-finite values.
Results may differ from the reference program's by a relative error of at most 0.005.
Values may be sent and summed in bfloat16 or wider, within the bound.
No kernel may reach another device: no remote copies, remote signals or barrier semaphores. Data moves between devices by JAX's collectives and lax.ppermute only.
A program may use at most 128 MiB of HBM per device.

```python
import math
import jax
import jax.numpy as jnp
from jax import lax

D = 12288
FF = 12288
TOKENS = 2048


def draw_tokens(key, part):
    key = jax.random.fold_in(key, 11)
    first_key, second_key, third_key = jax.random.split(key, 3)
    row_scale = jnp.exp(jax.random.uniform(second_key, (TOKENS, 1), jnp.float32, math.log(0.3), math.log(3.0)))
    column_scale = jnp.exp(jax.random.uniform(third_key, (1, D), jnp.float32, math.log(0.3), math.log(3.0)))
    base_draw = jnp.clip(jax.random.normal(first_key, (TOKENS, D), jnp.float32), -3.5, 3.5)
    return (base_draw * row_scale * column_scale).astype(jnp.bfloat16)


def block_levels(key, shape, pieces, least, top_value):
    gain, own = 1.0, jax.random.fold_in(key, 6)
    for dim, parts in pieces:
        draws = jnp.exp(jax.random.uniform(jax.random.fold_in(own, dim), (parts,), jnp.float32, least / len(pieces), top_value / len(pieces)))
        gain = gain * jnp.repeat(draws, shape[dim] // parts).reshape([-1 if axis == dim else 1 for axis in range(len(shape))])
    return gain


def centred(stream_key, shape, spread, limit, shards=(), held_as=jnp.bfloat16):
    gain = block_levels(stream_key, shape, shards, -0.22, 0.18) if shards else 1.0
    array = jax.random.normal(stream_key, shape, jnp.float32) * spread * gain
    return jnp.minimum(jnp.maximum(array, -limit), limit).astype(held_as)


def setup_inputs(seed: int = 0) -> dict:
    key_list = jax.random.split(jax.random.key(seed), 6)
    return {
        "tokens": draw_tokens(jax.random.fold_in(key_list[5], 71), 0),
        "norm_gain": jnp.clip(1.0 + 0.18 * jax.random.normal(key_list[1], (D,), jnp.float32), 0.1, 1.9),
        "gate_weight": centred(key_list[2], (D, FF), D ** -0.5, 0.0546875, ((0, 16), (1, 16))),
        "up_weight": centred(key_list[3], (D, FF), D ** -0.5, 0.0546875, ((0, 16), (1, 16))),
        "down_weight": centred(key_list[4], (FF, D), (FF // 4) ** -0.5, 0.109375, ((0, 16), (1, 16))),
    }


def reference(tokens, norm_gain, gate_weight, up_weight, down_weight):
    inputs = tokens.astype(jnp.float32)
    inverse_rms = jax.lax.rsqrt(lax.optimization_barrier(jnp.mean(inputs * inputs, axis=1, keepdims=True)) + 1e-05)
    normed = (inputs * inverse_rms * norm_gain.astype(jnp.float32)).astype(jnp.bfloat16)
    gate = jnp.dot(normed, gate_weight, preferred_element_type=jnp.float32)
    up_values = jnp.dot(normed, up_weight, preferred_element_type=jnp.float32)
    hidden = (jax.nn.silu(gate) * up_values).astype(jnp.bfloat16)
    branch = jnp.dot(hidden, down_weight, preferred_element_type=jnp.float32)
    return (inputs + branch).astype(jnp.bfloat16)
```

```python
import jax
import jax.numpy as jnp
from jax import lax
from jax.sharding import Mesh, PartitionSpec as P

epsilon = 1e-05
f32, bf16 = jnp.float32, jnp.bfloat16
axes = ("yl", "x", "c", "yh", "z")


def product(left, right):
    return jnp.dot(left, right, preferred_element_type=f32)


def shift(block, steps):
    return lax.ppermute(block, "z", [(i, (i + steps) % 8) for i in range(8)])


def core_partner(block):
    return lax.ppermute(block, "c", [(0, 1), (1, 0)])


def y_partner(block, flip):
    return lax.ppermute(block, ("yl", "yh"), [(i, i ^ flip) for i in range(4)])


def swap_where(flag, array, axis):
    return jnp.where(flag, jnp.flip(array, axis), array)


def on_device(tokens, norm_gain, gate_weight, up_weight, down_weight):
    yl, core, yh, z = (lax.axis_index(name) for name in ("yl", "c", "yh", "z"))
    unit = gate_weight.shape[1]

    first = jnp.concatenate((gate_weight, up_weight), axis=1)
    first = jnp.concatenate((first, core_partner(first)), axis=0)
    second = jnp.concatenate(
        (
            jnp.concatenate((down_weight, y_partner(down_weight, 2)), axis=1),
            jnp.concatenate((y_partner(down_weight, 1), y_partner(down_weight, 3)), axis=1),
        ),
        axis=0,
    )
    second = jnp.concatenate((second, core_partner(second)), axis=1)

    inputs = tokens.astype(f32)
    inverse_rms = lax.rsqrt(jnp.mean(inputs * inputs, axis=1, keepdims=True) + epsilon)
    normed = (inputs * inverse_rms * norm_gain).astype(bf16)

    pieces = swap_where(core == 1, normed.reshape(8, 8, 2, unit), 2).reshape(8, 8, 2 * unit)
    pieces = jnp.broadcast_to(pieces.transpose(1, 0, 2)[:, None], (8, 2, 8, 2 * unit))
    block = lax.all_to_all(pieces.reshape(16, 8, 2 * unit), ("yl", "x", "yh"), 0, 0)
    block = block.reshape(128, 2 * unit)

    r1, l1 = shift(block, 1), shift(block, -1)
    r2, l2 = shift(r1, 1), shift(l1, -1)
    r3, l3 = shift(r2, 1), shift(l2, -1)
    opposite = jnp.concatenate((shift(r2[:64], 2), shift(l2[64:], -2)), axis=0)
    panel = jnp.stack(
        [piece.reshape(8, 16, 2 * unit) for piece in (block, r1, r2, r3, opposite, l3, l2, l1)],
        axis=1,
    )
    partial = product(panel.reshape(1024, 2 * unit), first).astype(bf16)
    terms = lax.all_to_all(partial.reshape(8, 128, 2 * unit), ("yl", "x"), 0, 0)
    summed = jnp.sum(terms.astype(f32), axis=0)
    hidden = (jax.nn.silu(summed[:, :unit]) * summed[:, unit:]).astype(bf16)

    hidden = jnp.flip(hidden.reshape(8, 2, 8, unit), 0)
    hidden = lax.dynamic_slice_in_dim(jnp.concatenate((hidden, hidden), axis=0), 7 - z, 8, axis=0)
    hidden = hidden.transpose(1, 0, 2, 3)[None]
    hidden = jnp.broadcast_to(hidden, (4, 2, 8, 8, unit)).reshape(8, 8, 8, unit)
    hidden = lax.all_to_all(hidden, ("x", "yh"), 0, 0).reshape(4, 2, 8, 8, unit)
    hidden = swap_where(yh == 1, hidden, 1)
    hidden = hidden.transpose(2, 0, 3, 1, 4).reshape(256, 2 * unit)

    branch = product(hidden, second).astype(bf16)
    terms = lax.all_to_all(branch.reshape(8, 32, 4 * unit), "z", 0, 0)
    branch = jnp.sum(terms.astype(f32), axis=0).astype(bf16)
    branch = lax.all_to_all(branch.reshape(4, 8, 4 * unit), "x", 0, 0)
    branch = branch.reshape(4, 8, 2, 2, unit)
    branch = swap_where(core == 1, swap_where(yl == 1, branch, 3), 2)
    branch = branch.transpose(1, 3, 0, 2, 4).reshape(8, 16 * unit)
    return (inputs + branch.astype(f32)).astype(bf16)


def solution(mesh):
    grid = Mesh(mesh.devices.reshape(2, 4, 2, 2, 8), axes)
    row, col = ("yl", "x", "c"), ("yh", "z")
    return jax.shard_map(
        on_device,
        mesh=grid,
        in_specs=(P(axes, None), P(), P(row, col), P(row, col), P(col, row)),
        out_specs=P(axes, None),
        check_vma=False,
    )
```

```python
import jax
import jax.numpy as jnp
from jax import lax
from jax.experimental import pallas as pl
from jax.experimental.pallas import tpu as pltpu
from jax.sharding import Mesh, PartitionSpec as P

epsilon = 1e-05
f32, bf16 = jnp.float32, jnp.bfloat16
axes = ("yl", "x", "c", "yh", "z")
unit = 768
tile = 256
room = 24 * 2**20
anywhere = pl.BlockSpec(memory_space=pl.ANY)


def product(left, right):
    return jnp.dot(left, right, preferred_element_type=f32)


def shift(block, steps):
    return lax.ppermute(block, "z", [(i, (i + steps) % 8) for i in range(8)])


def core_partner(block):
    return lax.ppermute(block, "c", [(0, 1), (1, 0)])


def yh_partner(block):
    return lax.ppermute(block, "yh", [(0, 1), (1, 0)])


def swap_where(flag, array, axis):
    return jnp.where(flag, jnp.flip(array, axis), array)


def nothing(array, dependency, out):
    pass


def after(dependency, array):
    return pl.pallas_call(
        nothing,
        in_specs=[anywhere, anywhere],
        out_specs=anywhere,
        out_shape=jax.ShapeDtypeStruct(array.shape, array.dtype),
        input_output_aliases={0: 0},
    )(array, dependency)


def first_kernel(count, *refs):
    blocks, (own, other, _, out, panel) = refs[:count], refs[count:]

    @pl.when(pl.program_id(0) == 0)
    def _():
        for s, block in enumerate(blocks):
            for j in range(8):
                panel[j, s] = block[16 * j : 16 * (j + 1)]

    rows = panel[...].reshape(128 * count, 2 * unit)
    total = product(rows[:, :unit], own[...]) + product(rows[:, unit:], other[...])
    out[...] = total.astype(bf16).reshape(8, 16 * count, tile)


def first_product(blocks, own, other, dependency):
    count = len(blocks)
    weight_spec = pl.BlockSpec((unit, tile), lambda j: (0, j))
    return pl.pallas_call(
        lambda *refs: first_kernel(count, *refs),
        grid=(2 * unit // tile,),
        in_specs=[pl.BlockSpec((128, 2 * unit), lambda j: (0, 0))] * count
        + [weight_spec, weight_spec, anywhere],
        out_specs=pl.BlockSpec((8, 16 * count, tile), lambda j: (0, 0, j)),
        out_shape=pltpu.HBM((8, 16 * count, 2 * unit), bf16),
        scratch_shapes=[pltpu.VMEM((8, count, 16, 2 * unit), bf16)],
        compiler_params=pltpu.CompilerParams(vmem_limit_bytes=room),
        cost_estimate=pl.CostEstimate(
            flops=count * 128 * 8 * unit * unit,
            bytes_accessed=8 * unit * unit,
            transcendentals=0,
        ),
    )(*blocks, own, other, dependency)


def second_kernel(hidden, own, other, own_y, other_y, near, left, right, left_half, right_half):
    places = {0: near.at[0], 2: near.at[1], 6: near.at[2]}
    places |= {1: left.at[0], 3: left.at[1], 7: right.at[0], 5: right.at[1]}
    for n, (weight, weight_y) in enumerate(((own, own_y), (other, other_y))):
        total = product(hidden[0], weight[...]) + product(hidden[1], weight_y[...])
        total = total.astype(bf16).reshape(8, 64, tile)
        for s, place in places.items():
            place[n] = total[s]
        (left_half, right_half)[n][...] = total[4]


def second_product(hidden, weights):
    counts = (3, 2, 2)
    return pl.pallas_call(
        second_kernel,
        grid=(unit // tile,),
        in_specs=[pl.BlockSpec((2, 512, unit), lambda j: (0, 0, 0))]
        + [pl.BlockSpec((unit, tile), lambda j: (0, j))] * 4,
        out_specs=[pl.BlockSpec((k, 2, 64, tile), lambda j: (0, 0, 0, j)) for k in counts]
        + [pl.BlockSpec((64, tile), lambda j: (0, j))] * 2,
        out_shape=[jax.ShapeDtypeStruct((k, 2, 64, unit), bf16) for k in counts]
        + [jax.ShapeDtypeStruct((64, unit), bf16)] * 2,
        compiler_params=pltpu.CompilerParams(vmem_limit_bytes=room),
        cost_estimate=pl.CostEstimate(
            flops=512 * 8 * unit * unit, bytes_accessed=8 * unit * unit, transcendentals=0
        ),
    )(hidden, *weights)


def relay_kernel(near, left, right, left_half, right_half, to_left, to_right):
    for n in range(2):
        a = near[1, n].astype(f32) + left[1, n].astype(f32)
        b = near[2, n].astype(f32) + right[1, n].astype(f32)
        if n == 0:
            a += left_half[...].astype(f32)
        else:
            b += right_half[...].astype(f32)
        to_left[n] = a.astype(bf16)
        to_right[n] = b.astype(bf16)


def relay(*arrays):
    return pl.pallas_call(
        relay_kernel, out_shape=[jax.ShapeDtypeStruct((2, 64, unit), bf16)] * 2
    )(*arrays)


def on_device(tokens, norm_gain, gate_weight, up_weight, down_weight):
    core, yh = lax.axis_index("c"), lax.axis_index("yh")

    inputs = tokens.astype(f32)
    inverse_rms = lax.rsqrt(jnp.mean(inputs * inputs, axis=1, keepdims=True) + epsilon)
    normed = (inputs * inverse_rms * norm_gain).astype(bf16)
    pieces = swap_where(core == 1, normed.reshape(8, 8, 2, unit), 2).reshape(8, 8, 2 * unit)
    pieces = jnp.broadcast_to(pieces.transpose(1, 0, 2)[:, None], (8, 2, 8, 2 * unit))
    block = lax.all_to_all(pieces.reshape(16, 8, 2 * unit), ("yl", "x", "yh"), 0, 0)
    block = block.reshape(128, 2 * unit)

    first = jnp.concatenate((gate_weight, up_weight), axis=1)
    first_other = core_partner(first)

    r1, l1 = shift(block, 1), shift(block, -1)
    r2, l2 = shift(r1, 1), shift(l1, -1)
    r3, l3 = shift(r2, 1), shift(l2, -1)
    opposite = jnp.concatenate((shift(r2[:64], 2), shift(l2[64:], -2)), axis=0)

    down_y = yh_partner(after(block, down_weight))
    blocks = (block, r1, r2, r3, opposite, l3, l2, l1)
    partial = first_product(blocks, first, first_other, down_y)
    terms = lax.all_to_all(partial, ("yl", "x"), 0, 0)

    down_y = after(partial, down_y)
    weights = (down_weight, core_partner(down_weight), down_y, core_partner(down_y))

    summed = jnp.sum(terms.astype(f32), axis=0)
    hidden = (jax.nn.silu(summed[:, :unit]) * summed[:, unit:]).astype(bf16)
    hidden = hidden.reshape(8, 2, 8, unit)

    hidden = hidden.transpose(1, 0, 2, 3)[None]
    hidden = jnp.broadcast_to(hidden, (8, 2, 8, 8, unit)).reshape(16, 64, unit)
    hidden = lax.all_to_all(hidden, ("yl", "x", "yh"), 0, 0).reshape(8, 2, 8, 8, unit)
    hidden = swap_where(yh == 1, hidden, 1)
    hidden = hidden.transpose(1, 2, 0, 3, 4).reshape(2, 512, unit)

    mine, left, right, left_half, right_half = second_product(hidden, weights)
    left, right = shift(left, -1), shift(right, 1)
    left_half, right_half = shift(left_half, -2), shift(right_half, 2)
    to_left, to_right = relay(mine, left, right, left_half, right_half)
    terms = (mine[0], left[0], right[0], shift(to_left, -2), shift(to_right, 2))
    branch = sum(term.astype(f32) for term in terms).astype(bf16)

    branch = branch.reshape(2, 8, 8, unit).transpose(1, 0, 2, 3)
    branch = lax.all_to_all(branch.reshape(8, 16, unit), ("yl", "x"), 0, 0)
    branch = swap_where(core == 1, branch.reshape(8, 2, 8, unit), 1)
    branch = branch.transpose(2, 0, 1, 3).reshape(8, 16 * unit)
    return (tokens.astype(f32) + branch.astype(f32)).astype(bf16)


def solution(mesh):
    grid = Mesh(mesh.devices.reshape(2, 4, 2, 2, 8), axes)
    row, col = ("yl", "x", "c"), ("yh", "z")
    return jax.shard_map(
        on_device,
        mesh=grid,
        in_specs=(P(axes, None), P(), P(row, col), P(row, col), P(col, row)),
        out_specs=P(axes, None),
        check_vma=False,
    )
```

```python
import jax
import jax.numpy as jnp
from jax import lax
from jax.experimental import pallas as pl
from jax.experimental.pallas import tpu as pltpu
from jax.sharding import Mesh, PartitionSpec as P

epsilon = 1e-05
f32, bf16 = jnp.float32, jnp.bfloat16
axes = ("yl", "x", "c", "yh", "z")
unit = 768
tile = 256
room = 24 * 2**20
anywhere = pl.BlockSpec(memory_space=pl.ANY)


def in_hbm(array):
    return pltpu.with_memory_space_constraint(array, pltpu.HBM)


def product(left, right):
    return jnp.dot(left, right, preferred_element_type=f32)


def shift(block, steps):
    return lax.ppermute(block, "z", [(i, (i + steps) % 8) for i in range(8)])


def core_partner(block):
    return lax.ppermute(block, "c", [(0, 1), (1, 0)])


def yh_partner(block):
    return lax.ppermute(block, "yh", [(0, 1), (1, 0)])


def swap_where(flag, array, axis):
    return jnp.where(flag, jnp.flip(array, axis), array)


def nothing(array, dependency, out):
    pass


def after(dependency, array):
    return pl.pallas_call(
        nothing,
        in_specs=[anywhere, anywhere],
        out_specs=anywhere,
        out_shape=jax.ShapeDtypeStruct(array.shape, array.dtype),
        input_output_aliases={0: 0},
        compiler_params=pltpu.CompilerParams(vmem_limit_bytes=2**20),
    )(array, dependency)


def first_kernel(rows, *refs):
    pieces, weight, (out, panel) = refs[: len(rows)], refs[len(rows)], refs[-2:]

    @pl.when(pl.program_id(0) == 0)
    def _():
        for (s, first_row), piece in zip(rows, pieces):
            for j in range(piece.shape[0] // 16):
                panel[first_row // 16 + j, s] = piece[16 * j : 16 * (j + 1)]

    total = product(panel[...].reshape(512, 2 * unit), weight[0])
    out[...] = total.astype(bf16).reshape(8, 64, unit)


def first_product(rows, pieces, weight, *beside):
    half = len(beside) // 2
    return pl.pallas_call(
        lambda *refs: first_kernel(rows, *refs),
        grid=(2,),
        in_specs=[pl.BlockSpec(piece.shape, lambda i: (0, 0)) for piece in pieces]
        + [pl.BlockSpec((1, 2 * unit, unit), lambda i: (i, 0, 0))]
        + [anywhere] * len(beside),
        out_specs=pl.BlockSpec((8, 64, unit), lambda i: (0, half, i)),
        out_shape=pltpu.HBM((8, 128, 2 * unit), bf16),
        input_output_aliases={len(rows) + 1: 0} if half else {},
        scratch_shapes=[pltpu.VMEM((8, 4, 16, 2 * unit), bf16)],
        compiler_params=pltpu.CompilerParams(vmem_limit_bytes=room),
        cost_estimate=pl.CostEstimate(
            flops=512 * 8 * unit * unit, bytes_accessed=8 * unit * unit, transcendentals=0
        ),
    )(*pieces, weight, *beside)


def stack_kernel(a, b, c, d, out):
    out[0, :unit], out[0, unit:], out[1, :unit], out[1, unit:] = a[...], b[...], c[...], d[...]


def stack(*weights):
    return pl.pallas_call(
        stack_kernel,
        grid=(3,),
        in_specs=[pl.BlockSpec((unit, tile), lambda j: (0, j))] * 4,
        out_specs=pl.BlockSpec((2, 2 * unit, tile), lambda j: (0, 0, j)),
        out_shape=jax.ShapeDtypeStruct((2, 2 * unit, unit), bf16),
        compiler_params=pltpu.CompilerParams(vmem_limit_bytes=8 * 2**20),
    )(*(in_hbm(weight) for weight in weights))


order = (0, 1, 7, 2, 6, 3, 5, 4)


def second_kernel(_, mine, theirs, weight, near, left, right, left_half, right_half):
    places = {0: near.at[0], 2: near.at[1], 6: near.at[2]}
    places |= {1: left.at[0], 3: left.at[1], 7: right.at[0], 5: right.at[1]}
    total = product(mine[...].reshape(512, unit), weight[0, :unit])
    total += product(theirs[...].reshape(512, unit), weight[0, unit:])
    total = total.reshape(8, 8, 8, unit)
    for k, s in enumerate(order):
        piece = total[:, k].reshape(64, unit).astype(bf16)
        if s != 4:
            places[s][0] = piece
            continue
        for n, half in enumerate((left_half, right_half)):

            @pl.when(pl.program_id(0) == n)
            def _(half=half, piece=piece):
                half[...] = piece


def second_product(yh, hidden, weight):
    counts = (3, 2, 2)
    return pl.pallas_call(
        second_kernel,
        grid_spec=pltpu.PrefetchScalarGridSpec(
            num_scalar_prefetch=1,
            grid=(2,),
            in_specs=[
                pl.BlockSpec((8, 1, 64, unit), lambda n, yh: (0, yh[0], 0, 0)),
                pl.BlockSpec((8, 1, 64, unit), lambda n, yh: (0, 1 - yh[0], 0, 0)),
                pl.BlockSpec((1, 2 * unit, unit), lambda n, yh: (n, 0, 0)),
            ],
            out_specs=[pl.BlockSpec((k, 1, 64, unit), lambda n, yh: (0, n, 0, 0)) for k in counts]
            + [pl.BlockSpec((64, unit), lambda n, yh: (0, 0))] * 2,
        ),
        out_shape=[jax.ShapeDtypeStruct((k, 2, 64, unit), bf16) for k in counts]
        + [jax.ShapeDtypeStruct((64, unit), bf16)] * 2,
        compiler_params=pltpu.CompilerParams(vmem_limit_bytes=room),
        cost_estimate=pl.CostEstimate(
            flops=512 * 8 * unit * unit, bytes_accessed=8 * unit * unit, transcendentals=0
        ),
    )(yh.reshape(1), hidden, hidden, weight)


def relay_kernel(near, left, right, left_half, right_half, to_left, to_right):
    for n in range(2):
        a = near[1, n].astype(f32) + left[1, n].astype(f32)
        b = near[2, n].astype(f32) + right[1, n].astype(f32)
        if n == 0:
            a += left_half[...].astype(f32)
        else:
            b += right_half[...].astype(f32)
        to_left[n] = a.astype(bf16)
        to_right[n] = b.astype(bf16)


def relay(*arrays):
    return pl.pallas_call(
        relay_kernel,
        out_shape=[jax.ShapeDtypeStruct((2, 64, unit), bf16)] * 2,
        compiler_params=pltpu.CompilerParams(vmem_limit_bytes=6 * 2**20),
    )(*arrays)


def prepare_kernel(core, tokens, norm_gain, out):
    inputs = tokens[...].astype(f32)
    inverse_rms = lax.rsqrt(jnp.mean(inputs * inputs, axis=1, keepdims=True) + epsilon)
    normed = inputs * inverse_rms * norm_gain[...]
    swap = core[0] == 1
    for j in range(8):
        low = normed[:, 2 * j * unit : (2 * j + 1) * unit]
        high = normed[:, (2 * j + 1) * unit : (2 * j + 2) * unit]
        for y in range(2):
            out[j, y, :, :unit] = jnp.where(swap, high, low).astype(bf16)
            out[j, y, :, unit:] = jnp.where(swap, low, high).astype(bf16)


def prepare(core, tokens, norm_gain):
    vmem = pl.BlockSpec(memory_space=pltpu.VMEM)
    return pl.pallas_call(
        prepare_kernel,
        in_specs=[pl.BlockSpec(memory_space=pltpu.SMEM), vmem, vmem],
        out_specs=vmem,
        out_shape=pltpu.HBM((8, 2, 8, 2 * unit), bf16),
        compiler_params=pltpu.CompilerParams(vmem_limit_bytes=8 * 2**20),
    )(core.reshape(1), in_hbm(tokens), in_hbm(norm_gain.reshape(1, -1)))


def on_device(tokens, norm_gain, gate_weight, up_weight, down_weight):
    core, yh = lax.axis_index("c"), lax.axis_index("yh")

    pieces = prepare(core, tokens, norm_gain)
    block = lax.all_to_all(pieces.reshape(16, 8, 2 * unit), ("yl", "x", "yh"), 0, 0)
    block = block.reshape(128, 2 * unit)

    r1, l1 = shift(block, 1), shift(block, -1)
    r2, l2 = shift(r1, 1), shift(l1, -1)
    r3, l3 = shift(r2, 1), shift(l2, -1)
    r4, l4 = shift(r2[:64], 2), shift(l2[64:], -2)

    first = stack(
        gate_weight, core_partner(gate_weight), up_weight, core_partner(up_weight)
    )
    down_y = yh_partner(after(block, down_weight))
    whole = [(s, 0) for s in range(4)]
    partial = first_product(whole, (block, r1, l1, r2), first)
    far = [(0, 0), (1, 0), (2, 0), (3, 0), (3, 64)]
    partial = first_product(far, (l2, r3, l3, r4, l4), first, partial, down_y)
    terms = lax.all_to_all(partial, ("yl", "x"), 0, 0)

    down_y = after(partial, down_y)
    second = stack(down_weight, down_y, core_partner(down_weight), core_partner(down_y))

    summed = jnp.sum(terms.astype(f32), axis=0)
    hidden = (jax.nn.silu(summed[:, :unit]) * summed[:, unit:]).astype(bf16)

    hidden = hidden.reshape(8, 2, 8, unit).transpose(1, 0, 2, 3)[None]
    hidden = jnp.broadcast_to(hidden, (8, 2, 8, 8, unit)).reshape(16, 64, unit)
    hidden = lax.all_to_all(hidden, ("yl", "x", "yh"), 0, 0).reshape(8, 2, 64, unit)

    mine, left, right, left_half, right_half = second_product(yh, hidden, second)
    left, right = shift(left, -1), shift(right, 1)
    left_half, right_half = shift(left_half, -2), shift(right_half, 2)
    to_left, to_right = relay(mine, left, right, left_half, right_half)
    terms = (mine[0], left[0], right[0], shift(to_left, -2), shift(to_right, 2))
    branch = sum(term.astype(f32) for term in terms).astype(bf16)

    branch = branch.reshape(2, 8, 8, unit).transpose(1, 0, 2, 3)
    branch = lax.all_to_all(branch.reshape(8, 16, unit), ("yl", "x"), 0, 0)
    branch = swap_where(core == 1, branch.reshape(8, 2, 8, unit), 1)
    branch = branch.transpose(2, 0, 1, 3).reshape(8, 16 * unit)
    return (tokens.astype(f32) + branch.astype(f32)).astype(bf16)


def solution(mesh):
    grid = Mesh(mesh.devices.reshape(2, 4, 2, 2, 8), axes)
    row, col = ("yl", "x", "c"), ("yh", "z")
    return jax.shard_map(
        on_device,
        mesh=grid,
        in_specs=(P(axes, None), P(), P(row, col), P(row, col), P(col, row)),
        out_specs=P(axes, None),
        check_vma=False,
    )
```

```python
import jax
import jax.numpy as jnp
from jax import lax
from jax.experimental import pallas as pl
from jax.experimental.pallas import tpu as pltpu
from jax.sharding import Mesh, PartitionSpec as P

epsilon = 1e-05
f32, bf16 = jnp.float32, jnp.bfloat16
axes = ("yl", "x", "c", "yh", "z")
unit = 768
tile = 256
room = 24 * 2**20
anywhere = pl.BlockSpec(memory_space=pl.ANY)


def in_hbm(array):
    return pltpu.with_memory_space_constraint(array, pltpu.HBM)


def product(left, right):
    return jnp.dot(left, right, preferred_element_type=f32)


def shift(block, steps):
    return lax.ppermute(block, "z", [(i, (i + steps) % 8) for i in range(8)])


def core_partner(block):
    return lax.ppermute(block, "c", [(0, 1), (1, 0)])


def yh_partner(block):
    return lax.ppermute(block, "yh", [(0, 1), (1, 0)])


def swap_where(flag, array, axis):
    return jnp.where(flag, jnp.flip(array, axis), array)


def nothing(array, dependency, out):
    pass


def after(dependency, array):
    return pl.pallas_call(
        nothing,
        in_specs=[anywhere, anywhere],
        out_specs=anywhere,
        out_shape=jax.ShapeDtypeStruct(array.shape, array.dtype),
        input_output_aliases={0: 0},
        compiler_params=pltpu.CompilerParams(vmem_limit_bytes=2**20),
    )(array, dependency)


def first_kernel(rows, *refs):
    pieces, weight, (out, panel) = refs[: len(rows)], refs[len(rows)], refs[-2:]

    @pl.when(pl.program_id(0) == 0)
    def _():
        for (s, first_row), piece in zip(rows, pieces):
            for j in range(piece.shape[0] // 16):
                panel[first_row // 16 + j, s] = piece[16 * j : 16 * (j + 1)]

    total = product(panel[...].reshape(512, 2 * unit), weight[0])
    total = total.reshape(8, 4, 2, 8, unit)
    for y in range(2):
        out[:, y] = total[:, :, y].reshape(8, 32, unit).astype(bf16)


def first_product(rows, pieces, weight, *beside):
    half = len(beside) // 2
    return pl.pallas_call(
        lambda *refs: first_kernel(rows, *refs),
        grid=(2,),
        in_specs=[pl.BlockSpec(piece.shape, lambda i: (0, 0)) for piece in pieces]
        + [pl.BlockSpec((1, 2 * unit, unit), lambda i: (i, 0, 0))]
        + [anywhere] * len(beside),
        out_specs=pl.BlockSpec((8, 2, 32, unit), lambda i: (0, 0, half, i)),
        out_shape=pltpu.HBM((8, 2, 64, 2 * unit), bf16),
        input_output_aliases={len(rows) + 1: 0} if half else {},
        scratch_shapes=[pltpu.VMEM((8, 4, 16, 2 * unit), bf16)],
        compiler_params=pltpu.CompilerParams(vmem_limit_bytes=room),
        cost_estimate=pl.CostEstimate(
            flops=512 * 8 * unit * unit, bytes_accessed=8 * unit * unit, transcendentals=0
        ),
    )(*pieces, weight, *beside)


def stack_kernel(a, b, c, d, out):
    out[0, :unit], out[0, unit:], out[1, :unit], out[1, unit:] = a[...], b[...], c[...], d[...]


def stack(shape, *weights):
    return pl.pallas_call(
        stack_kernel,
        grid=(3,),
        in_specs=[pl.BlockSpec((unit, tile), lambda j: (0, j))] * 4,
        out_specs=pl.BlockSpec((2, 2 * unit, tile), lambda j: (0, 0, j)),
        out_shape=shape((2, 2 * unit, unit), bf16),
        compiler_params=pltpu.CompilerParams(vmem_limit_bytes=8 * 2**20),
    )(*(in_hbm(weight) for weight in weights))


order = (0, 1, 7, 2, 6, 3, 5, 4)


def second_kernel(_, mine, theirs, weight, near, left, right, p1, p7, left_half, right_half):
    places = {0: near.at[0], 2: near.at[1], 6: near.at[2]}
    places |= {3: left.at[0], 5: right.at[0], 1: p1.at[0], 7: p7.at[0]}
    total = product(mine[...].reshape(512, unit), weight[0, :unit])
    total += product(theirs[...].reshape(512, unit), weight[0, unit:])
    total = total.reshape(8, 8, 8, unit)
    for k, s in enumerate(order):
        piece = total[:, k].reshape(64, unit).astype(bf16)
        if s != 4:
            places[s][0] = piece
            continue
        for n, half in enumerate((left_half, right_half)):

            @pl.when(pl.program_id(0) == n)
            def _(half=half, piece=piece):
                half[...] = piece


def second_product(yh, hidden, weight):
    counts = (3, 1, 1, 1, 1)
    return pl.pallas_call(
        second_kernel,
        grid_spec=pltpu.PrefetchScalarGridSpec(
            num_scalar_prefetch=1,
            grid=(2,),
            in_specs=[
                pl.BlockSpec((8, 1, 64, unit), lambda n, yh: (0, yh[0], 0, 0)),
                pl.BlockSpec((8, 1, 64, unit), lambda n, yh: (0, 1 - yh[0], 0, 0)),
                pl.BlockSpec((1, 2 * unit, unit), lambda n, yh: (n, 0, 0)),
            ],
            out_specs=[pl.BlockSpec((k, 1, 64, unit), lambda n, yh: (0, n, 0, 0)) for k in counts]
            + [pl.BlockSpec((64, unit), lambda n, yh: (0, 0))] * 2,
        ),
        out_shape=[jax.ShapeDtypeStruct((k, 2, 64, unit), bf16) for k in counts]
        + [jax.ShapeDtypeStruct((64, unit), bf16)] * 2,
        compiler_params=pltpu.CompilerParams(vmem_limit_bytes=room),
        cost_estimate=pl.CostEstimate(
            flops=512 * 8 * unit * unit, bytes_accessed=8 * unit * unit, transcendentals=0
        ),
    )(yh.reshape(1), hidden, hidden, in_hbm(weight))


def relay_kernel(near, left, right, left_half, right_half, to_left, to_right):
    for n in range(2):
        a = near[1, n].astype(f32) + left[0, n].astype(f32)
        b = near[2, n].astype(f32) + right[0, n].astype(f32)
        if n == 0:
            a += left_half[...].astype(f32)
        else:
            b += right_half[...].astype(f32)
        to_left[n] = a.astype(bf16)
        to_right[n] = b.astype(bf16)


def relay(*arrays):
    return pl.pallas_call(
        relay_kernel,
        out_shape=[jax.ShapeDtypeStruct((2, 64, unit), bf16)] * 2,
        compiler_params=pltpu.CompilerParams(vmem_limit_bytes=6 * 2**20),
    )(*arrays)


def prepare_kernel(core, tokens, norm_gain, out):
    inputs = tokens[...].astype(f32)
    inverse_rms = lax.rsqrt(jnp.mean(inputs * inputs, axis=1, keepdims=True) + epsilon)
    normed = inputs * inverse_rms * norm_gain[...]
    swap = core[0] == 1
    for j in range(8):
        low = normed[:, 2 * j * unit : (2 * j + 1) * unit]
        high = normed[:, (2 * j + 1) * unit : (2 * j + 2) * unit]
        for y in range(2):
            out[j, y, :, :unit] = jnp.where(swap, high, low).astype(bf16)
            out[j, y, :, unit:] = jnp.where(swap, low, high).astype(bf16)


def prepare(core, tokens, norm_gain):
    vmem = pl.BlockSpec(memory_space=pltpu.VMEM)
    return pl.pallas_call(
        prepare_kernel,
        in_specs=[pl.BlockSpec(memory_space=pltpu.SMEM), vmem, vmem],
        out_specs=vmem,
        out_shape=pltpu.HBM((8, 2, 8, 2 * unit), bf16),
        compiler_params=pltpu.CompilerParams(vmem_limit_bytes=8 * 2**20),
    )(core.reshape(1), in_hbm(tokens), in_hbm(norm_gain.reshape(1, -1)))


def on_device(tokens, norm_gain, gate_weight, up_weight, down_weight):
    core, yh = lax.axis_index("c"), lax.axis_index("yh")

    pieces = prepare(core, tokens, norm_gain)
    block = lax.all_to_all(pieces.reshape(16, 8, 2 * unit), ("yl", "x", "yh"), 0, 0)
    block = block.reshape(128, 2 * unit)

    r1, l1 = shift(block, 1), shift(block, -1)
    r2, l2 = shift(r1, 1), shift(l1, -1)
    r3, l3 = shift(r2, 1), shift(l2, -1)
    r4, l4 = shift(r2[:64], 2), shift(l2[64:], -2)

    first = (gate_weight, core_partner(gate_weight), up_weight, core_partner(up_weight))
    first = stack(jax.ShapeDtypeStruct, *first)
    down_y = yh_partner(after(block, down_weight))
    whole = [(s, 0) for s in range(4)]
    partial = first_product(whole, (block, r1, l1, r2), first)
    far = [(0, 0), (1, 0), (2, 0), (3, 0), (3, 64)]
    partial = first_product(far, (l2, r3, l3, r4, l4), first, partial, down_y)
    terms = lax.all_to_all(partial.reshape(16, 64, 2 * unit), ("yl", "x", "yh"), 0, 0)

    down_y = after(in_hbm(partial), down_y)
    second = (down_weight, down_y, core_partner(down_weight), core_partner(down_y))
    second = stack(pltpu.HBM, *second)

    summed = jnp.sum(terms.reshape(8, 2, 64, 2 * unit).astype(f32), axis=0)
    hidden = (jax.nn.silu(summed[:, :, :unit]) * summed[:, :, unit:]).astype(bf16)

    hidden = jnp.broadcast_to(hidden[None], (8, 2, 64, unit))
    hidden = lax.all_to_all(hidden, ("yl", "x"), 0, 0)

    mine, left, right, p1, p7, left_half, right_half = second_product(yh, hidden, second)
    left_half, right_half = shift(left_half, -2), shift(right_half, 2)
    left, right = shift(left, -1), shift(right, 1)
    p1, p7 = shift(p1, -1), shift(p7, 1)
    to_left, to_right = relay(mine, left, right, left_half, right_half)
    terms = (mine[0], p1[0], p7[0], shift(to_left, -2), shift(to_right, 2))
    branch = sum(term.astype(f32) for term in terms).astype(bf16)

    branch = branch.reshape(2, 8, 8, unit).transpose(1, 0, 2, 3)
    branch = lax.all_to_all(branch.reshape(8, 16, unit), ("yl", "x"), 0, 0)
    branch = swap_where(core == 1, branch.reshape(8, 2, 8, unit), 1)
    branch = branch.transpose(2, 0, 1, 3).reshape(8, 16 * unit)
    return (tokens.astype(f32) + branch.astype(f32)).astype(bf16)


def solution(mesh):
    grid = Mesh(mesh.devices.reshape(2, 4, 2, 2, 8), axes)
    row, col = ("yl", "x", "c"), ("yh", "z")
    return jax.shard_map(
        on_device,
        mesh=grid,
        in_specs=(P(axes, None), P(), P(row, col), P(row, col), P(col, row)),
        out_specs=P(axes, None),
        check_vma=False,
    )
```

```python
import jax
import jax.numpy as jnp
from jax import lax
from jax.experimental import pallas as pl
from jax.experimental.pallas import tpu as pltpu
from jax.sharding import Mesh, PartitionSpec as P

epsilon = 1e-05
f32, bf16 = jnp.float32, jnp.bfloat16
axes = ("yl", "x", "c", "yh", "z")
unit = 768
tile = 256
room = 24 * 2**20
anywhere = pl.BlockSpec(memory_space=pl.ANY)


def in_hbm(array):
    return pltpu.with_memory_space_constraint(array, pltpu.HBM)


def product(left, right):
    return jnp.dot(left, right, preferred_element_type=f32)


def shift(block, steps):
    return lax.ppermute(block, "z", [(i, (i + steps) % 8) for i in range(8)])


def core_partner(block):
    return lax.ppermute(block, "c", [(0, 1), (1, 0)])


def yh_partner(block):
    return lax.ppermute(block, "yh", [(0, 1), (1, 0)])


def swap_where(flag, array, axis):
    return jnp.where(flag, jnp.flip(array, axis), array)


def nothing(array, dependency, out):
    pass


def after(dependency, array):
    return pl.pallas_call(
        nothing,
        in_specs=[anywhere, anywhere],
        out_specs=anywhere,
        out_shape=jax.ShapeDtypeStruct(array.shape, array.dtype),
        input_output_aliases={0: 0},
        compiler_params=pltpu.CompilerParams(vmem_limit_bytes=2**20),
    )(array, dependency)


def first_kernel(rows, *refs):
    pieces, weight, (out, panel) = refs[: len(rows)], refs[len(rows)], refs[-2:]

    @pl.when(pl.program_id(0) == 0)
    def _():
        for (s, first_row), piece in zip(rows, pieces):
            for j in range(piece.shape[0] // 16):
                panel[first_row // 16 + j, s] = piece[16 * j : 16 * (j + 1)]

    total = product(panel[...].reshape(512, 2 * unit), weight[0])
    total = total.reshape(8, 4, 2, 8, unit)
    for y in range(2):
        out[:, y] = total[:, :, y].reshape(8, 32, unit).astype(bf16)


def first_product(rows, pieces, weight, *beside):
    half = len(beside) // 2
    return pl.pallas_call(
        lambda *refs: first_kernel(rows, *refs),
        grid=(2,),
        in_specs=[pl.BlockSpec(piece.shape, lambda i: (0, 0)) for piece in pieces]
        + [pl.BlockSpec((1, 2 * unit, unit), lambda i: (i, 0, 0))]
        + [anywhere] * len(beside),
        out_specs=pl.BlockSpec((8, 2, 32, unit), lambda i: (0, 0, half, i)),
        out_shape=pltpu.HBM((8, 2, 64, 2 * unit), bf16),
        input_output_aliases={len(rows) + 1: 0} if half else {},
        scratch_shapes=[pltpu.VMEM((8, 4, 16, 2 * unit), bf16)],
        compiler_params=pltpu.CompilerParams(vmem_limit_bytes=room),
        cost_estimate=pl.CostEstimate(
            flops=512 * 8 * unit * unit, bytes_accessed=8 * unit * unit, transcendentals=0
        ),
    )(*pieces, weight, *beside)


def stack_kernel(a, b, c, d, out):
    out[0, :unit], out[0, unit:], out[1, :unit], out[1, unit:] = a[...], b[...], c[...], d[...]


def stack(*weights):
    return pl.pallas_call(
        stack_kernel,
        grid=(3,),
        in_specs=[pl.BlockSpec((unit, tile), lambda j: (0, j))] * 4,
        out_specs=pl.BlockSpec((2, 2 * unit, tile), lambda j: (0, 0, j)),
        out_shape=jax.ShapeDtypeStruct((2, 2 * unit, unit), bf16),
        compiler_params=pltpu.CompilerParams(vmem_limit_bytes=8 * 2**20),
    )(*(in_hbm(weight) for weight in weights))


order = (0, 1, 7, 2, 6, 3, 5, 4)


def activate_kernel(terms, out, hidden, sent):
    copies = []
    for y in range(2):
        total = terms[y].astype(f32)
        for j in range(1, 8):
            total += terms[2 * j + y].astype(f32)
        hidden[y] = (jax.nn.silu(total[:, :unit]) * total[:, unit:]).astype(bf16)
        for j in range(8):
            copies.append(pltpu.make_async_copy(hidden.at[y], out.at[j, y], sent.at[y, j]))
            copies[-1].start()
    for copy in copies:
        copy.wait()


def activate(terms):
    return pl.pallas_call(
        activate_kernel,
        in_specs=[pl.BlockSpec(memory_space=pltpu.VMEM)],
        out_specs=anywhere,
        out_shape=pltpu.HBM((8, 2, 64, unit), bf16),
        scratch_shapes=[pltpu.VMEM((2, 64, unit), bf16), pltpu.SemaphoreType.DMA((2, 8))],
        compiler_params=pltpu.CompilerParams(vmem_limit_bytes=12 * 2**20),
    )(terms)


def fetch(weights, held, arrived):
    return [
        pltpu.make_async_copy(
            weight, held.at[k // 2, pl.ds(k % 2 * unit, unit)], arrived.at[k]
        )
        for k, weight in enumerate(weights)
    ]


held_weights = [pltpu.VMEM((2, 2 * unit, unit), bf16), pltpu.SemaphoreType.DMA((4,))]


def second_kernel(_, mine, theirs, *refs):
    near, left, right, p1, p7, left_half, right_half, held, arrived = refs[4:]
    places = {0: near.at[0], 2: near.at[1], 6: near.at[2]}
    places |= {3: left.at[0], 5: right.at[0], 1: p1.at[0], 7: p7.at[0]}
    step = pl.program_id(0)
    copies = fetch(refs[:4], held, arrived)

    @pl.when(step == 0)
    def _():
        for copy in copies:
            copy.start()
        copies[0].wait()

    pl.when(step == 1)(copies[2].wait)
    total = product(mine[...].reshape(512, unit), held[step, :unit])
    pl.when(step == 0)(copies[1].wait)
    pl.when(step == 1)(copies[3].wait)
    total += product(theirs[...].reshape(512, unit), held[step, unit:])
    total = total.reshape(8, 8, 8, unit)
    for k, s in enumerate(order):
        piece = total[:, k].reshape(64, unit).astype(bf16)
        if s != 4:
            places[s][0] = piece
            continue
        for n, half in enumerate((left_half, right_half)):

            @pl.when(pl.program_id(0) == n)
            def _(half=half, piece=piece):
                half[...] = piece


def second_product(yh, hidden, weights):
    counts = (3, 1, 1, 1, 1)
    return pl.pallas_call(
        second_kernel,
        grid_spec=pltpu.PrefetchScalarGridSpec(
            num_scalar_prefetch=1,
            grid=(2,),
            in_specs=[
                pl.BlockSpec((8, 1, 64, unit), lambda n, yh: (0, yh[0], 0, 0)),
                pl.BlockSpec((8, 1, 64, unit), lambda n, yh: (0, 1 - yh[0], 0, 0)),
            ]
            + [anywhere] * 4,
            out_specs=[pl.BlockSpec((k, 1, 64, unit), lambda n, yh: (0, n, 0, 0)) for k in counts]
            + [pl.BlockSpec((64, unit), lambda n, yh: (0, 0))] * 2,
            scratch_shapes=held_weights,
        ),
        out_shape=[jax.ShapeDtypeStruct((k, 2, 64, unit), bf16) for k in counts]
        + [jax.ShapeDtypeStruct((64, unit), bf16)] * 2,
        compiler_params=pltpu.CompilerParams(vmem_limit_bytes=room),
        cost_estimate=pl.CostEstimate(
            flops=512 * 8 * unit * unit, bytes_accessed=8 * unit * unit, transcendentals=0
        ),
    )(yh.reshape(1), hidden, hidden, *(in_hbm(weight) for weight in weights))


def relay_kernel(near, left, right, left_half, right_half, to_left, to_right):
    for n in range(2):
        a = near[1, n].astype(f32) + left[0, n].astype(f32)
        b = near[2, n].astype(f32) + right[0, n].astype(f32)
        if n == 0:
            a += left_half[...].astype(f32)
        else:
            b += right_half[...].astype(f32)
        to_left[n] = a.astype(bf16)
        to_right[n] = b.astype(bf16)


def relay(*arrays):
    return pl.pallas_call(
        relay_kernel,
        out_shape=[jax.ShapeDtypeStruct((2, 64, unit), bf16)] * 2,
        compiler_params=pltpu.CompilerParams(vmem_limit_bytes=6 * 2**20),
    )(*arrays)


def prepare_kernel(core, tokens, norm_gain, out):
    inputs = tokens[...].astype(f32)
    inverse_rms = lax.rsqrt(jnp.mean(inputs * inputs, axis=1, keepdims=True) + epsilon)
    normed = inputs * inverse_rms * norm_gain[...]
    swap = core[0] == 1
    for j in range(8):
        low = normed[:, 2 * j * unit : (2 * j + 1) * unit]
        high = normed[:, (2 * j + 1) * unit : (2 * j + 2) * unit]
        for k, half in enumerate((jnp.where(swap, high, low), jnp.where(swap, low, high))):
            twice = jnp.concatenate((half, half), axis=0)
            out[j, :, k * unit : (k + 1) * unit] = twice.astype(bf16)


def prepare(core, tokens, norm_gain):
    vmem = pl.BlockSpec(memory_space=pltpu.VMEM)
    return pl.pallas_call(
        prepare_kernel,
        in_specs=[pl.BlockSpec(memory_space=pltpu.SMEM), vmem, vmem],
        out_specs=vmem,
        out_shape=pltpu.HBM((8, 16, 2 * unit), bf16),
        compiler_params=pltpu.CompilerParams(vmem_limit_bytes=8 * 2**20),
    )(core.reshape(1), in_hbm(tokens), in_hbm(norm_gain.reshape(1, -1)))


def on_device(tokens, norm_gain, gate_weight, up_weight, down_weight):
    core, yh = lax.axis_index("c"), lax.axis_index("yh")

    pieces = prepare(core, tokens, norm_gain)
    block = lax.all_to_all(pieces.reshape(16, 8, 2 * unit), ("yl", "x", "yh"), 0, 0)
    block = block.reshape(128, 2 * unit)

    r1, l1 = shift(block, 1), shift(block, -1)
    r2, l2 = shift(r1, 1), shift(l1, -1)
    r3, l3 = shift(r2, 1), shift(l2, -1)
    r4, l4 = shift(r2[:64], 2), shift(l2[64:], -2)

    first = (gate_weight, core_partner(gate_weight), up_weight, core_partner(up_weight))
    first = stack(*first)
    down_y = yh_partner(after(block, down_weight))
    whole = [(s, 0) for s in range(4)]
    partial = first_product(whole, (block, r1, l1, r2), first)
    far = [(0, 0), (1, 0), (2, 0), (3, 0), (3, 64)]
    partial = first_product(far, (l2, r3, l3, r4, l4), first, partial, down_y)
    terms = lax.all_to_all(partial.reshape(16, 64, 2 * unit), ("yl", "x", "yh"), 0, 0)

    down_y = after(in_hbm(partial), down_y)
    second = (down_weight, down_y, core_partner(down_weight), core_partner(down_y))

    hidden = activate(terms)
    hidden = lax.all_to_all(hidden, ("yl", "x"), 0, 0)

    mine, left, right, p1, p7, left_half, right_half = second_product(yh, hidden, second)
    left, right = shift(left, -1), shift(right, 1)
    left_half, right_half = shift(left_half, -2), shift(right_half, 2)
    p1, p7 = shift(p1, -1), shift(p7, 1)
    to_left, to_right = relay(mine, left, right, left_half, right_half)
    terms = (mine[0], p1[0], p7[0], shift(to_left, -2), shift(to_right, 2))
    branch = sum(term.astype(f32) for term in terms).astype(bf16)

    branch = branch.reshape(2, 8, 8, unit).transpose(1, 0, 2, 3)
    branch = lax.all_to_all(branch.reshape(8, 16, unit), ("yl", "x"), 0, 0)
    branch = swap_where(core == 1, branch.reshape(8, 2, 8, unit), 1)
    branch = branch.transpose(2, 0, 1, 3).reshape(8, 16 * unit)
    return (tokens.astype(f32) + branch.astype(f32)).astype(bf16)


def solution(mesh):
    grid = Mesh(mesh.devices.reshape(2, 4, 2, 2, 8), axes)
    row, col = ("yl", "x", "c"), ("yh", "z")
    return jax.shard_map(
        on_device,
        mesh=grid,
        in_specs=(P(axes, None), P(), P(row, col), P(row, col), P(col, row)),
        out_specs=P(axes, None),
        check_vma=False,
    )
```

```python
import jax
import jax.numpy as jnp
from jax import lax
from jax.experimental import pallas as pl
from jax.experimental.pallas import tpu as pltpu
from jax.sharding import Mesh, PartitionSpec as P

epsilon = 1e-05
f32, bf16 = jnp.float32, jnp.bfloat16
axes = ("yl", "x", "c", "yh", "z")
unit = 768
tile = 256
room = 24 * 2**20
anywhere = pl.BlockSpec(memory_space=pl.ANY)


def in_hbm(array):
    return pltpu.with_memory_space_constraint(array, pltpu.HBM)


def product(left, right):
    return jnp.dot(left, right, preferred_element_type=f32)


def shift(block, steps):
    return lax.ppermute(block, "z", [(i, (i + steps) % 8) for i in range(8)])


def core_partner(block):
    return lax.ppermute(block, "c", [(0, 1), (1, 0)])


def yh_partner(block):
    return lax.ppermute(block, "yh", [(0, 1), (1, 0)])


def swap_where(flag, array, axis):
    return jnp.where(flag, jnp.flip(array, axis), array)


def nothing(array, dependency, out):
    pass


def after(dependency, array):
    return pl.pallas_call(
        nothing,
        in_specs=[anywhere, anywhere],
        out_specs=anywhere,
        out_shape=jax.ShapeDtypeStruct(array.shape, array.dtype),
        input_output_aliases={0: 0},
        compiler_params=pltpu.CompilerParams(vmem_limit_bytes=2**20),
    )(array, dependency)


def first_kernel(rows, *refs):
    pieces, weight, (out, panel) = refs[: len(rows)], refs[len(rows)], refs[-2:]

    @pl.when(pl.program_id(0) == 0)
    def _():
        for (s, first_row), piece in zip(rows, pieces):
            for j in range(piece.shape[0] // 16):
                panel[first_row // 16 + j, s] = piece[16 * j : 16 * (j + 1)]

    total = product(panel[...].reshape(512, 2 * unit), weight[0])
    total = total.reshape(8, 4, 2, 8, unit)
    for y in range(2):
        out[:, y] = total[:, :, y].reshape(8, 32, unit).astype(bf16)


def first_product(rows, pieces, weight, *beside):
    half = len(beside) // 2
    return pl.pallas_call(
        lambda *refs: first_kernel(rows, *refs),
        grid=(2,),
        in_specs=[pl.BlockSpec(piece.shape, lambda i: (0, 0)) for piece in pieces]
        + [pl.BlockSpec((1, 2 * unit, unit), lambda i: (i, 0, 0))]
        + [anywhere] * len(beside),
        out_specs=pl.BlockSpec((8, 2, 32, unit), lambda i: (0, 0, half, i)),
        out_shape=jax.ShapeDtypeStruct((8, 2, 64, 2 * unit), bf16),
        input_output_aliases={len(rows) + 1: 0} if half else {},
        scratch_shapes=[pltpu.VMEM((8, 4, 16, 2 * unit), bf16)],
        compiler_params=pltpu.CompilerParams(vmem_limit_bytes=room),
        cost_estimate=pl.CostEstimate(
            flops=512 * 8 * unit * unit, bytes_accessed=8 * unit * unit, transcendentals=0
        ),
    )(*pieces, weight, *beside)


def stack_kernel(a, b, c, d, out):
    out[0, :unit], out[0, unit:], out[1, :unit], out[1, unit:] = a[...], b[...], c[...], d[...]


def stack(*weights):
    return pl.pallas_call(
        stack_kernel,
        grid=(3,),
        in_specs=[pl.BlockSpec((unit, tile), lambda j: (0, j))] * 4,
        out_specs=pl.BlockSpec((2, 2 * unit, tile), lambda j: (0, 0, j)),
        out_shape=jax.ShapeDtypeStruct((2, 2 * unit, unit), bf16),
        compiler_params=pltpu.CompilerParams(vmem_limit_bytes=8 * 2**20),
    )(*(in_hbm(weight) for weight in weights))


order = (0, 1, 7, 2, 6, 3, 5, 4)


def activate_kernel(terms, out, hidden, sent):
    copies = []
    for y in range(2):
        total = terms[y].astype(f32)
        for j in range(1, 8):
            total += terms[2 * j + y].astype(f32)
        hidden[y] = (jax.nn.silu(total[:, :unit]) * total[:, unit:]).astype(bf16)
        for j in range(8):
            copies.append(pltpu.make_async_copy(hidden.at[y], out.at[j, y], sent.at[y, j]))
            copies[-1].start()
    for copy in copies:
        copy.wait()


def activate(terms):
    return pl.pallas_call(
        activate_kernel,
        in_specs=[pl.BlockSpec(memory_space=pltpu.VMEM)],
        out_specs=anywhere,
        out_shape=pltpu.HBM((8, 2, 64, unit), bf16),
        scratch_shapes=[pltpu.VMEM((2, 64, unit), bf16), pltpu.SemaphoreType.DMA((2, 8))],
        compiler_params=pltpu.CompilerParams(vmem_limit_bytes=12 * 2**20),
    )(terms)


def fetch(weights, held, arrived):
    return [
        pltpu.make_async_copy(
            weight, held.at[k // 2, pl.ds(k % 2 * unit, unit)], arrived.at[k]
        )
        for k, weight in enumerate(weights)
    ]


held_weights = [pltpu.VMEM((2, 2 * unit, unit), bf16), pltpu.SemaphoreType.DMA((4,))]


def second_kernel(_, mine, theirs, *refs):
    near, left, right, p1, p7, left_half, right_half, held, arrived = refs[4:]
    places = {0: near.at[0], 2: near.at[1], 6: near.at[2]}
    places |= {3: left.at[0], 5: right.at[0], 1: p1.at[0], 7: p7.at[0]}
    step = pl.program_id(0)
    copies = fetch(refs[:4], held, arrived)

    @pl.when(step == 0)
    def _():
        for copy in copies:
            copy.start()
        copies[0].wait()

    pl.when(step == 1)(copies[2].wait)
    total = product(mine[...].reshape(512, unit), held[step, :unit])
    pl.when(step == 0)(copies[1].wait)
    pl.when(step == 1)(copies[3].wait)
    total += product(theirs[...].reshape(512, unit), held[step, unit:])
    total = total.reshape(8, 8, 8, unit)
    for k, s in enumerate(order):
        piece = total[:, k].reshape(64, unit).astype(bf16)
        if s != 4:
            places[s][0] = piece
            continue
        for n, half in enumerate((left_half, right_half)):

            @pl.when(pl.program_id(0) == n)
            def _(half=half, piece=piece):
                half[...] = piece


def second_product(yh, hidden, weights):
    counts = (3, 1, 1, 1, 1)
    return pl.pallas_call(
        second_kernel,
        grid_spec=pltpu.PrefetchScalarGridSpec(
            num_scalar_prefetch=1,
            grid=(2,),
            in_specs=[
                pl.BlockSpec((8, 1, 64, unit), lambda n, yh: (0, yh[0], 0, 0)),
                pl.BlockSpec((8, 1, 64, unit), lambda n, yh: (0, 1 - yh[0], 0, 0)),
            ]
            + [anywhere] * 4,
            out_specs=[pl.BlockSpec((k, 1, 64, unit), lambda n, yh: (0, n, 0, 0)) for k in counts]
            + [pl.BlockSpec((64, unit), lambda n, yh: (0, 0))] * 2,
            scratch_shapes=held_weights,
        ),
        out_shape=[jax.ShapeDtypeStruct((k, 2, 64, unit), bf16) for k in counts]
        + [jax.ShapeDtypeStruct((64, unit), bf16)] * 2,
        compiler_params=pltpu.CompilerParams(vmem_limit_bytes=room),
        cost_estimate=pl.CostEstimate(
            flops=512 * 8 * unit * unit, bytes_accessed=8 * unit * unit, transcendentals=0
        ),
    )(yh.reshape(1), hidden, hidden, *(in_hbm(weight) for weight in weights))


def relay_kernel(near, left, right, left_half, right_half, to_left, to_right):
    for n in range(2):
        a = near[1, n].astype(f32) + left[0, n].astype(f32)
        b = near[2, n].astype(f32) + right[0, n].astype(f32)
        if n == 0:
            a += left_half[...].astype(f32)
        else:
            b += right_half[...].astype(f32)
        to_left[n] = a.astype(bf16)
        to_right[n] = b.astype(bf16)


def relay(*arrays):
    return pl.pallas_call(
        relay_kernel,
        out_shape=[jax.ShapeDtypeStruct((2, 64, unit), bf16)] * 2,
        compiler_params=pltpu.CompilerParams(vmem_limit_bytes=6 * 2**20),
    )(*arrays)


def prepare_kernel(core, tokens, norm_gain, out):
    inputs = tokens[...].astype(f32)
    inverse_rms = lax.rsqrt(jnp.mean(inputs * inputs, axis=1, keepdims=True) + epsilon)
    normed = inputs * inverse_rms * norm_gain[...]
    swap = core[0] == 1
    for j in range(8):
        low = normed[:, 2 * j * unit : (2 * j + 1) * unit]
        high = normed[:, (2 * j + 1) * unit : (2 * j + 2) * unit]
        for k, half in enumerate((jnp.where(swap, high, low), jnp.where(swap, low, high))):
            twice = jnp.concatenate((half, half), axis=0)
            out[j, :, k * unit : (k + 1) * unit] = twice.astype(bf16)


def prepare(core, tokens, norm_gain):
    vmem = pl.BlockSpec(memory_space=pltpu.VMEM)
    return pl.pallas_call(
        prepare_kernel,
        in_specs=[pl.BlockSpec(memory_space=pltpu.SMEM), vmem, vmem],
        out_specs=vmem,
        out_shape=pltpu.HBM((8, 16, 2 * unit), bf16),
        compiler_params=pltpu.CompilerParams(vmem_limit_bytes=8 * 2**20),
    )(core.reshape(1), in_hbm(tokens), in_hbm(norm_gain.reshape(1, -1)))


def on_device(tokens, norm_gain, gate_weight, up_weight, down_weight):
    core, yh = lax.axis_index("c"), lax.axis_index("yh")

    pieces = prepare(core, tokens, norm_gain)
    block = lax.all_to_all(pieces.reshape(16, 8, 2 * unit), ("yl", "x", "yh"), 0, 0)
    block = block.reshape(128, 2 * unit)

    r1, l1 = shift(block, 1), shift(block, -1)
    r2, l2 = shift(r1, 1), shift(l1, -1)
    r3, l3 = shift(r2, 1), shift(l2, -1)
    r4, l4 = shift(r2[:64], 2), shift(l2[64:], -2)

    first = (gate_weight, core_partner(gate_weight), up_weight, core_partner(up_weight))
    first = stack(*first)
    down_y = yh_partner(after(block, down_weight))
    whole = [(s, 0) for s in range(4)]
    partial = first_product(whole, (block, r1, l1, r2), first)
    far = [(0, 0), (1, 0), (2, 0), (3, 0), (3, 64)]
    partial = first_product(far, (l2, r3, l3, r4, l4), first, partial, down_y)
    terms = lax.all_to_all(partial.reshape(16, 64, 2 * unit), ("yl", "x", "yh"), 0, 0)

    hidden = activate(terms)

    down_y = after(in_hbm(hidden), down_y)
    second = (down_weight, down_y, core_partner(down_weight), core_partner(down_y))
    hidden = lax.all_to_all(hidden, ("yl", "x"), 0, 0)

    mine, left, right, p1, p7, left_half, right_half = second_product(yh, hidden, second)
    left, right = shift(left, -1), shift(right, 1)
    left_half, right_half = shift(left_half, -2), shift(right_half, 2)
    p1, p7 = shift(p1, -1), shift(p7, 1)
    to_left, to_right = relay(mine, left, right, left_half, right_half)
    terms = (mine[0], p1[0], p7[0], shift(to_left, -2), shift(to_right, 2))
    branch = sum(term.astype(f32) for term in terms).astype(bf16)

    branch = branch.reshape(2, 8, 8, unit).transpose(1, 0, 2, 3)
    branch = lax.all_to_all(branch.reshape(8, 16, unit), ("yl", "x"), 0, 0)
    branch = swap_where(core == 1, branch.reshape(8, 2, 8, unit), 1)
    branch = branch.transpose(2, 0, 1, 3).reshape(8, 16 * unit)
    return (tokens.astype(f32) + branch.astype(f32)).astype(bf16)


def solution(mesh):
    grid = Mesh(mesh.devices.reshape(2, 4, 2, 2, 8), axes)
    row, col = ("yl", "x", "c"), ("yh", "z")
    return jax.shard_map(
        on_device,
        mesh=grid,
        in_specs=(P(axes, None), P(), P(row, col), P(row, col), P(col, row)),
        out_specs=P(axes, None),
        check_vma=False,
    )
```
